256 devices in a mesh: seq: 32 (over x, z), expert: 8 (over y, core).
Axes of the slice: x: 4, y: 4, z: 8, core: 2. Of those that a mesh axis runs over, the one named last changes fastest.
Arguments:
- tokens: bfloat16 [2, 16384, 4096], P(None, ('seq', 'expert')), may hold values from -12 to 12
- routes: int32 [2, 16384, 4], P(None, 'seq'), may hold values from 0 to 31, all different within a row; in each aligned block of 64 rows (0 to 63, 64 to 127, ..., all dimensions but the last counted through in order) at most 12 rows name the same one
- gates: float32 [2, 16384, 4], P(None, ('seq', 'expert')), may hold values from 0.2 to 3
- w_kv: bfloat16 [4096, 256], replicated, may hold values from -0.6 to 0.6
- w_query: bfloat16 [32, 4096, 128], P('expert'), may hold values from -0.6 to 0.6
- w_out: bfloat16 [32, 128, 4096], P('expert'), may hold values from -0.5 to 0.5
Outputs:
- mixed: bfloat16 [2, 16384, 4096], P(None, ('seq', 'expert'))
- balance: float32 [], replicated
The draws below stay inside these ranges and needn't reach their ends.
Inputs may be any that keep to these rules, and one draw needn't show every extreme that they name: In each aligned block of 64 positions of a sequence no head expert is named by more than 12 routes, and some head expert by exactly 12; a position names 4 different head experts.
All inputs are finite; a program needn't handle non-finite values.
Results may differ from the reference program's by a relative error of at most 0.01.
The reference program's roundings to bfloat16 on the way count: a program that leaves them out, or rounds other values in their place, can miss the bound.
Values may be sent and summed in bfloat16 or wider, within the bound.
No kernel may reach another device: no remote copies, remote signals or barrier semaphores. Data moves between devices by JAX's collectives and lax.ppermute only.
A program may use at most 128 MiB of HBM per device.

```python
import math
import jax
import jax.numpy as jnp
import numpy as np
from jax import lax

D = 4096
HD = 128
TOP = 4
BATCH = 2
SEQ_DEV = 64
E = 32
L = 16384
MOST = 12
N_SEQ = 32
N_EXPERT = 8


def base_keys(key):
    return jax.random.normal(key, (D, HD), jnp.float32) * D ** (-0.5)


def draw_w_kv(key, part):
    shared = base_keys(key)
    key = jax.random.fold_in(key, 11)
    values = jax.random.normal(key, (D, HD), jnp.float32) * D ** (-0.5)
    joined = jnp.concatenate([shared, values], axis=1)
    return jnp.clip(joined, -0.6, 0.6).astype(jnp.bfloat16)


def draw_w_query(key, part):
    key = jax.random.fold_in(key, 12)
    noise = jax.random.normal(key, (E, D, HD), jnp.float32) * D ** (-0.5)
    return jnp.clip(noise, -0.6, 0.6).astype(jnp.bfloat16)


def draw_tokens(key, part):
    key = jax.random.fold_in(key, 13)
    ramp = 1.0 + 1.5 * (1.0 - jnp.arange(L, dtype=jnp.float32) / L)
    values = jax.random.normal(key, (BATCH, L, D), jnp.float32) * ramp[None, :, None]
    return jnp.clip(values, -12.0, 12.0).astype(jnp.bfloat16)


def draw_gates(key, part):
    key = jax.random.fold_in(key, 14)
    ramp = 1.0 + 2.0 * jnp.arange(L, dtype=jnp.float32) / L
    base = jax.random.uniform(key, (BATCH, L, TOP), jnp.float32, 0.2, 1.0)
    return base * ramp[None, :, None]


def block_scale(own_key, extent, pieces, low, largest):
    loudness = 1.0
    for dim, parts in pieces:
        heights = jax.random.uniform(jax.random.fold_in(jax.random.fold_in(own_key, 6), dim), (parts,), jnp.float32, low / len(pieces), largest / len(pieces))
        loudness = loudness * jnp.repeat(jnp.exp(heights), extent[dim] // parts).reshape((-1,) + (1,) * (len(extent) - 1 - dim))
    return loudness


def deal_out(stream_key, own, number, rows, count, top, bound, slope):
    order = jax.random.permutation(stream_key, count)
    crowded, common = load_shares(count, rows * top, bound, slope, True), load_shares(count, rows * top, bound, slope, False)
    places = jnp.arange(count)

    def named(lengths, turn):
        used = int((lengths > 0).sum())
        fixed = max(1, used // 4)
        shifted = fixed + (places - fixed + turn * (used - fixed)) % max(1, count - fixed)
        return jnp.zeros((count,), jnp.int32).at[order[jnp.where(places < fixed, places, shifted)]].set(jnp.asarray(lengths, jnp.int32))

    lengths = jnp.where(number % 4 == 0, named(crowded, number // 4), named(common, number - number // 4 - 1))
    mixed = jax.random.permutation(jax.random.fold_in(own, 3), count)
    source_of, sink = mixed[0:count // 2 * 2:2], mixed[1:count // 2 * 2:2]
    margin = jnp.minimum(lengths[source_of] - 1, bound - lengths[sink]) // 2
    margin = jnp.where((source_of == order[0]) | (sink == order[0]) | (lengths[sink] == 0), 0, jnp.maximum(margin, 0))
    shifted = jax.random.randint(jax.random.fold_in(own, 4), (count // 2,), 0, 1 << 20) % (margin + 1)
    lengths = lengths.at[source_of].add(-shifted).at[sink].add(shifted)
    members = jnp.searchsorted(jnp.cumsum(lengths), jnp.arange(rows * top), side="right").astype(jnp.int32)
    grid = members.reshape(top, rows).T
    grid = grid[jax.random.permutation(jax.random.fold_in(own, 1), rows)]
    turn = jax.random.randint(jax.random.fold_in(own, 2), (rows, 1), 0, top)
    return jnp.take_along_axis(grid, (jnp.arange(top)[None, :] + turn) % top, axis=1)


def load_shares(count, total, bound, skew, full):
    portions = [(1 << 20) // math.isqrt(grade ** skew) + 1 for grade in range(1, count + 1)]
    largest = bound if full else min(bound, max(-(-total // count), total * portions[0] // sum(portions)))
    least = 1 if total - largest >= count - 1 else 0
    holding, surplus = [largest] + [least] * (count - 1), total - largest - least * (count - 1)
    while surplus > 0:
        candidates = [i for i in range(1, count) if holding[i] < largest] or [i for i in range(1, count) if holding[i] < bound]
        pool, budget = sum([portions[i] for i in candidates]), surplus
        for i in candidates:
            extra = min(bound - holding[i], max(1, budget * portions[i] // pool), surplus)
            holding[i] = holding[i] + extra
            surplus = surplus - extra
    return np.array(holding)


def scatter_about(own_key, dims, width, limit, split=(), held_as=jnp.bfloat16):
    drawn = jax.random.normal(own_key, dims, jnp.float32) * width
    if len(split) > 0:
        drawn = block_scale(own_key, dims, split, -0.22, 0.18) * drawn
    return jnp.clip(drawn, min=-limit, max=limit).astype(held_as)


def setup_inputs(seed: int = 0) -> dict:
    key_of = jax.random.split(jax.random.key(seed), 7)
    tokens = draw_tokens(jax.random.fold_in(key_of[6], 71), 0)
    routes_keys = jax.random.split(jax.random.fold_in(key_of[1], 1), BATCH * L // SEQ_DEV)
    routes_turns = jax.random.permutation(jax.random.fold_in(key_of[1], 3), BATCH * L // SEQ_DEV)
    routes = jax.vmap(lambda own, number: deal_out(jax.random.fold_in(key_of[1], 2), own, number, SEQ_DEV, E, TOP, MOST, 2))(routes_keys, routes_turns).reshape((BATCH, L, TOP))
    gates = draw_gates(jax.random.fold_in(key_of[6], 71), 0)
    w_kv = draw_w_kv(jax.random.fold_in(key_of[6], 71), 0)
    w_query = draw_w_query(jax.random.fold_in(key_of[6], 71), 0)
    w_out = scatter_about(key_of[5], (E, HD, D), HD ** -0.5, 0.5, ((0, 8),))
    return dict(tokens=tokens, routes=routes, gates=gates, w_kv=w_kv, w_query=w_query, w_out=w_out)


def slot_table(block_ids):
    rows = block_ids.shape[0]
    flat = block_ids.reshape(-1)
    onehot = (flat[:, None] == jnp.arange(E, dtype=jnp.int32)[None, :]).astype(jnp.int32)
    rank = jnp.cumsum(onehot, axis=0) - onehot
    slots = lax.optimization_barrier(jnp.sum(rank * onehot, axis=1))
    levels = jnp.arange(MOST, dtype=jnp.int32)
    match = onehot[:, :, None] * (slots[:, None, None] == levels[None, None, :]).astype(jnp.int32)
    owner = jnp.arange(rows * TOP, dtype=jnp.int32) // TOP + 1
    table = lax.optimization_barrier(jnp.sum(match * owner[:, None, None], axis=0)) - 1
    return (slots.reshape(rows, TOP), table)

def attend(carry, query_rows, positions, key_rows, key_pos, scale):
    best, total, acc = carry
    scores = jnp.dot(query_rows, key_rows[:, :HD].T, preferred_element_type=jnp.float32) * scale
    causal_visible_mask = key_pos[None, :] <= positions[:, None]
    top_score = lax.optimization_barrier(jnp.max(jnp.where(causal_visible_mask, scores, -1e+30), axis=1))
    fresh = jnp.maximum(best, top_score)
    weights = jnp.where(causal_visible_mask, jnp.exp(scores - fresh[:, None]), 0.0)
    decay = jnp.exp(best - fresh)
    total = total * decay + lax.optimization_barrier(jnp.sum(weights, axis=1))
    acc = acc * decay[:, None] + jnp.dot(weights.astype(jnp.bfloat16), key_rows[:, HD:], preferred_element_type=jnp.float32)
    return (fresh, total, acc)

def reference(tokens, routes, gates, w_kv, w_query, w_out):
    block_rows = SEQ_DEV * N_EXPERT
    scale = 1.0 / math.sqrt(HD)
    zero_index = jnp.int32(0)
    kv = jnp.dot(tokens.reshape(BATCH * L, D), w_kv, preferred_element_type=jnp.float32)
    kv = kv.astype(jnp.bfloat16).reshape(BATCH, L, 2 * HD)
    query_w = w_query.astype(jnp.float32)
    out_w = w_out.astype(jnp.float32)
    slot_count = N_EXPERT * MOST

    def one_block(index):
        index = index.astype(jnp.int32)
        batch_row = (index // N_SEQ).astype(jnp.int32)
        seq_block = (index % N_SEQ).astype(jnp.int32)
        start = (seq_block * block_rows).astype(jnp.int32)
        x_block = lax.dynamic_slice(tokens, (batch_row, start, zero_index), (1, block_rows, D))[0]
        ids = lax.dynamic_slice(routes, (batch_row, start, zero_index), (1, block_rows, TOP))[0]
        weights = lax.dynamic_slice(gates, (batch_row, start, zero_index), (1, block_rows, TOP))[0]
        slots, tables = jax.vmap(slot_table)(ids.reshape(N_EXPERT, SEQ_DEV, TOP))
        valid = tables >= 0
        rows = jnp.where(valid, tables, 0) + (jnp.arange(N_EXPERT, dtype=jnp.int32) * SEQ_DEV)[:, None, None]
        rows = rows.transpose(1, 0, 2).reshape(E, slot_count)
        live = valid.transpose(1, 0, 2).reshape(E, slot_count)
        picked = jnp.where(live[:, :, None], x_block[rows], jnp.zeros((), jnp.bfloat16))
        query_rows = jnp.einsum('end,edh->enh', picked.astype(jnp.float32), query_w).astype(jnp.bfloat16)
        query_rows = query_rows.reshape(E * slot_count, HD)
        positions = (start + rows).reshape(-1)
        keys_all = lax.dynamic_index_in_dim(kv, batch_row, 0, keepdims=False)
        count = E * slot_count
        init = (jnp.full((count,), -1e+30, jnp.float32), jnp.zeros((count,), jnp.float32), jnp.zeros((count, HD), jnp.float32))

        def step(block, carry):
            block = block.astype(jnp.int32)
            key_start = (block * block_rows).astype(jnp.int32)
            key_rows = lax.dynamic_slice_in_dim(keys_all, key_start, block_rows, 0)
            key_pos = key_start + jnp.arange(block_rows, dtype=jnp.int32)
            return attend(carry, query_rows, positions, key_rows, key_pos, scale)
        best, total, acc = lax.fori_loop(zero_index, seq_block + jnp.int32(1), step, init)
        heads = (acc / total[:, None]).astype(jnp.bfloat16).reshape(E, slot_count, HD)
        projected = jnp.einsum('enh,ehd->end', heads.astype(jnp.float32), out_w).astype(jnp.bfloat16)
        projected = projected.reshape(E * slot_count, D)
        local = jnp.arange(block_rows, dtype=jnp.int32) // SEQ_DEV
        index_rows = ids * slot_count + local[:, None] * MOST + slots.reshape(block_rows, TOP)
        mixed = lax.optimization_barrier(jnp.sum(projected[index_rows].astype(jnp.float32) * weights[:, :, None], axis=1))
        return mixed.astype(jnp.bfloat16)
    mixed = lax.map(one_block, jnp.arange(BATCH * N_SEQ, dtype=jnp.int32)).reshape(BATCH, L, D)
    onehot = (routes[..., None] == jnp.arange(E, dtype=jnp.int32)).astype(jnp.float32)
    counts = lax.optimization_barrier(jnp.sum(onehot, axis=(0, 1, 2)))
    gate_sum = lax.optimization_barrier(jnp.sum(onehot * gates[..., None], axis=(0, 1, 2)))
    tokens_all = BATCH * L
    balance = E * jnp.sum(counts / (tokens_all * TOP) * (gate_sum / tokens_all))
    return (mixed, balance)
```

```python
import functools
import math

import jax
import jax.numpy as jnp
from jax import lax
from jax.experimental import pallas as pl
from jax.experimental.pallas import tpu as pltpu
from jax.sharding import PartitionSpec as P

BF = jnp.bfloat16
F32 = jnp.float32
VM = pltpu.VMEM
NX, NZ = 4, 8
NY, NC = 4, 2
NT = (((1,), (1,)), ((), ()))
TN = (((0,), (0,)), ((), ()))


def move_expert(v, step, flip):
    pairs = [
        (y * NC + c, ((y + step) % NY) * NC + (c ^ flip))
        for y in range(NY)
        for c in range(NC)
    ]
    return lax.ppermute(v, "expert", pairs)


def move_seq(v, dx, dz):
    pairs = [
        (x * NZ + z, ((x + dx) % NX) * NZ + (z + dz) % NZ)
        for x in range(NX)
        for z in range(NZ)
    ]
    return lax.ppermute(v, "seq", pairs)


def project(chunks, w_own, w_sib):
    rows = sum(c.shape[0] for c in chunks)
    width = chunks[0].shape[1]
    per, _, hd = w_own.shape
    n = len(chunks)

    def kernel(*refs):
        x = jnp.concatenate([r[...] for r in refs[:n]], axis=0)
        w = jnp.concatenate([refs[n][0], refs[n + 1][0]], axis=1)
        refs[n + 2][...] = jnp.dot(x, w, preferred_element_type=F32).astype(BF)

    return pl.pallas_call(
        kernel,
        grid=(per,),
        out_shape=jax.ShapeDtypeStruct((rows, 2 * per * hd), BF),
        in_specs=[pl.BlockSpec(c.shape, lambda i: (0, 0)) for c in chunks]
        + [pl.BlockSpec((1, width, hd), lambda i: (i, 0, 0))] * 2,
        out_specs=pl.BlockSpec((rows, 2 * hd), lambda i: (0, i)),
        compiler_params=pltpu.CompilerParams(vmem_limit_bytes=60 << 20),
        cost_estimate=pl.CostEstimate(
            flops=2 * rows * width * 2 * per * hd,
            bytes_accessed=2 * (rows * width + 2 * per * hd * width),
            transcendentals=0,
        ),
        name="project",
    )(*chunks, w_own, w_sib)


def expand(heads, first, pieces, w_own, w_sib, tile=1024, piece=64):
    per, hd, width = w_own.shape
    rows = piece * pieces

    def kernel(h_ref, wo_ref, ws_ref, *outs):
        h = h_ref[...]
        wo = wo_ref[...].reshape(per * hd, tile)
        ws = ws_ref[...].reshape(per * hd, tile)
        out = jnp.dot(h[:, : per * hd], wo, preferred_element_type=F32)
        out = out + jnp.dot(h[:, per * hd :], ws, preferred_element_type=F32)
        out = out.astype(BF)
        for k, ref in enumerate(outs):
            ref[...] = out[k * piece : (k + 1) * piece]

    return pl.pallas_call(
        kernel,
        grid=(width // tile,),
        out_shape=[jax.ShapeDtypeStruct((piece, width), BF)] * pieces,
        in_specs=[pl.BlockSpec((rows, 2 * per * hd), lambda i: (first, 0))]
        + [pl.BlockSpec((per, hd, tile), lambda i: (0, 0, i))] * 2,
        out_specs=[pl.BlockSpec((piece, tile), lambda i: (0, i))] * pieces,
        compiler_params=pltpu.CompilerParams(vmem_limit_bytes=60 << 20),
        cost_estimate=pl.CostEstimate(
            flops=2 * rows * width * 2 * per * hd,
            bytes_accessed=2 * (rows * width + 2 * per * hd * width),
            transcendentals=0,
        ),
        name="expand",
    )(heads, w_own, w_sib)


def compact(queries, slot_id, extra, most):
    n_q = len(queries)
    experts, tokens = slot_id.shape
    slots = 8 * most
    rows = experts * slots
    hd = queries[0].shape[1] // experts

    def kernel(*refs):
        q_refs = refs[:n_q]
        slot_ref, extra_ref, out_ref = refs[n_q:]
        level = lax.broadcasted_iota(jnp.int32, (slots, tokens), 0)
        for e in range(experts):
            pick = (level == slot_ref[e : e + 1, :]).astype(BF)
            col = (2 * e if e < experts // 2 else 2 * (e - experts // 2) + 1) * hd
            q = jnp.concatenate([r[:, col : col + hd] for r in q_refs], axis=0)
            out_ref[e * slots : (e + 1) * slots, :] = jnp.dot(
                pick, q, preferred_element_type=F32
            ).astype(BF)
        out_ref[rows:, :] = extra_ref[...]

    vm = pl.BlockSpec(memory_space=VM)
    return pl.pallas_call(
        kernel,
        out_shape=jax.ShapeDtypeStruct((rows + extra.shape[0], hd), BF),
        in_specs=[vm] * (n_q + 2),
        out_specs=vm,
        compiler_params=pltpu.CompilerParams(vmem_limit_bytes=60 << 20),
        cost_estimate=pl.CostEstimate(
            flops=2 * rows * tokens * hd, bytes_accessed=4 << 20, transcendentals=0
        ),
        name="compact",
    )(*queries, slot_id, extra)


def attention(order, queries, seen, pieces, rows, keys_in, tile=384, group=4):
    n_q = len(queries)
    n_p = len(pieces)
    hd = pieces[0].shape[-1] // 2
    blocks = sum(p.shape[0] for p in pieces)
    total = n_q * rows
    coef = math.log2(math.e) / math.sqrt(hd)
    lines = rows // hd

    def kernel(order_ref, *refs):
        q_refs = refs[:n_q]
        seen_ref = refs[n_q]
        piece_refs = refs[n_q + 1 : n_q + 1 + n_p]
        outs = refs[n_q + 1 + n_p : 2 * n_q + 1 + n_p]
        kv, tails, q_s, m_s, acc_s, sem, tail_sem = refs[2 * n_q + 1 + n_p :]
        copies = []
        late = []
        base = 0
        for k, ref in enumerate(piece_refs):
            size = ref.shape[0]
            copies.append(
                pltpu.make_async_copy(
                    ref.at[:, :keys_in, :], kv.at[base : base + size], sem.at[k]
                )
            )
            late.append(
                pltpu.make_async_copy(
                    ref.at[:, keys_in:, :], tails.at[base : base + size], tail_sem.at[k]
                )
            )
            base += size
        for copy in copies + late:
            copy.start()
        for k, ref in enumerate(q_refs):
            q_s[k * rows : (k + 1) * rows, :] = ref[:rows, :]
        for copy in copies:
            copy.wait()

        def fold(index, first):
            n = len(index)
            got = [kv[i] for i in index]
            keys = jnp.concatenate([a[:, :hd] for a in got], axis=0)
            vals = jnp.concatenate([a[:, hd:] for a in got], axis=0)
            vals = jnp.concatenate([vals, jnp.ones(vals.shape, BF)], axis=1)

            def several(t):
                if True:
                    at = pl.ds(t * tile, tile)
                    s = lax.dot_general(
                        q_s[at, :], keys, NT, preferred_element_type=F32
                    )
                    if first:
                        mask = seen_ref[at, :].astype(F32) > 0.5
                        head = jnp.where(mask, s[:, :keys_in], -1e30)
                        s = jnp.concatenate([head, s[:, keys_in:]], axis=1) if n > 1 else head
                    top = jnp.max(s, axis=1, keepdims=True)
                    if first:
                        new = jnp.broadcast_to(top, (tile, hd))
                    else:
                        old = m_s[at, :]
                        new = jnp.maximum(old, top)
                    wide = jnp.concatenate([new] * (n * keys_in // hd), axis=1)
                    p = jnp.exp2((s - wide) * coef)
                    if first:
                        head = jnp.where(mask, p[:, :keys_in], 0.0)
                        p = jnp.concatenate([head, p[:, keys_in:]], axis=1) if n > 1 else head
                    part = jnp.dot(p.astype(BF), vals, preferred_element_type=F32)
                    if not first:
                        decay = jnp.exp2((old - new) * coef)
                        part = part + acc_s[at, :] * jnp.concatenate([decay, decay], axis=1)
                    acc_s[at, :] = part
                    m_s[at, :] = new

            for t in range(total // tile):
                several(t)

        count = order_ref[blocks]
        extra = count % group
        for n in range(group):

            @pl.when(extra == n)
            def _(n=n):
                fold([0] + [order_ref[k] for k in range(n)], True)

        def step(i, carry):
            at = extra + i * group
            fold([order_ref[at + k] for k in range(group)], False)
            return carry

        lax.fori_loop(0, count // group, step, 0)

        eye = lax.broadcasted_iota(jnp.int32, (hd, hd), 0) == lax.broadcasted_iota(
            jnp.int32, (hd, hd), 1
        )
        which = lax.broadcasted_iota(jnp.int32, (8, hd), 0)
        for copy in late:
            copy.wait()
        sums = tails[0].astype(F32)
        for i in range(1, blocks):
            sums = sums + tails[i].astype(F32)
        sums = jnp.sum(sums, axis=0, keepdims=True)
        top = sums.astype(BF).astype(F32)
        mid = (sums - top).astype(BF).astype(F32)
        low = sums - top - mid
        note = jnp.zeros((8, hd), F32)
        for i, v in enumerate((top, mid, low)):
            note = jnp.where(which == 2 * i, v[:, :hd], note)
            note = jnp.where(which == 2 * i + 1, v[:, hd:], note)
        for k, ref in enumerate(outs):
            a = acc_s[k * rows : (k + 1) * rows, :]
            m = m_s[k * rows : (k + 1) * rows, :]
            amount = a[:, hd:]
            some = amount > 0.0
            safe = jnp.where(some, amount, 1.0)
            ref[:rows, :] = jnp.where(some, a[:, :hd] / safe, 0.0).astype(BF)
            level = jnp.where(some, m * coef + jnp.log2(safe), -1e30)
            flat = jnp.zeros((8, hd), F32)
            for i in range(lines):
                line = jnp.sum(
                    jnp.where(eye, level[i * hd : (i + 1) * hd, :], 0.0), axis=0, keepdims=True
                )
                flat = jnp.where(which == i, line, flat)
            hi = flat.astype(BF).astype(F32)
            mid = (flat - hi).astype(BF).astype(F32)
            low = flat - hi - mid
            ref[rows:, :] = jnp.concatenate([hi, mid, low, note], axis=0).astype(BF)

    vm = pl.BlockSpec(memory_space=VM)
    return pl.pallas_call(
        kernel,
        grid_spec=pltpu.PrefetchScalarGridSpec(
            num_scalar_prefetch=1,
            grid=(),
            in_specs=[vm] * (n_q + 1) + [pl.BlockSpec(memory_space=pl.ANY)] * n_p,
            out_specs=[vm] * n_q,
            scratch_shapes=[
                VM((blocks, keys_in, 2 * hd), BF),
                VM((blocks, pieces[0].shape[1] - keys_in, 2 * hd), BF),
                VM((total, hd), BF),
                VM((total, hd), F32),
                VM((total, 2 * hd), F32),
                pltpu.SemaphoreType.DMA((n_p,)),
                pltpu.SemaphoreType.DMA((n_p,)),
            ],
        ),
        out_shape=[jax.ShapeDtypeStruct((rows + 32, hd), BF)] * n_q,
        compiler_params=pltpu.CompilerParams(vmem_limit_bytes=60 << 20),
        cost_estimate=pl.CostEstimate(
            flops=total * blocks * keys_in * hd * 4,
            bytes_accessed=blocks * keys_in * hd * 4,
            transcendentals=total * blocks * keys_in,
        ),
        name="attention",
    )(order, *queries, seen, *pieces)


def merge(parts, slot_id, gate, most):
    n_q = len(parts)
    experts, tokens = slot_id.shape
    slots = 8 * most
    rows = experts * slots
    hd = parts[0].shape[1]
    lines = rows // hd

    def kernel(*refs):
        p_refs = refs[:n_q]
        slot_ref, gate_ref, out_ref, heads = refs[n_q:]
        eye = lax.broadcasted_iota(jnp.int32, (hd, hd), 0) == lax.broadcasted_iota(
            jnp.int32, (hd, hd), 1
        )
        levels = []
        for r in p_refs:
            tail = r[rows:, :].astype(F32)
            levels.append(tail[0:8] + tail[8:16] + tail[16:24])
        best = functools.reduce(jnp.maximum, levels)
        share = [jnp.exp2(v - best) for v in levels]
        amount = functools.reduce(jnp.add, share)
        share = [v / amount for v in share]
        for i in range(lines):
            at = slice(i * hd, (i + 1) * hd)
            out = jnp.zeros((hd, hd), F32)
            for r, v in zip(p_refs, share):
                w = jnp.sum(jnp.where(eye, v[i : i + 1, :], 0.0), axis=1, keepdims=True)
                out = out + w * r[at, :].astype(F32)
            heads[at, :] = out.astype(BF)
        level = lax.broadcasted_iota(jnp.int32, (slots, tokens), 0)
        for e in range(experts):
            pick = (level == slot_ref[e : e + 1, :]).astype(BF)
            spread = lax.dot_general(
                pick, heads[e * slots : (e + 1) * slots, :], TN, preferred_element_type=F32
            )
            out_ref[:, e * hd : (e + 1) * hd] = (spread * gate_ref[:, e : e + 1]).astype(BF)

    vm = pl.BlockSpec(memory_space=VM)
    return pl.pallas_call(
        kernel,
        out_shape=jax.ShapeDtypeStruct((tokens, experts * hd), BF),
        in_specs=[vm] * (n_q + 2),
        out_specs=vm,
        scratch_shapes=[VM((rows, hd), BF)],
        compiler_params=pltpu.CompilerParams(vmem_limit_bytes=60 << 20),
        cost_estimate=pl.CostEstimate(
            flops=2 * rows * tokens * hd, bytes_accessed=4 << 20, transcendentals=0
        ),
        name="merge",
    )(*parts, slot_id, gate)


def plan(where, ids, per, own_rows, most):
    top, tokens = ids.shape
    slots = NY * NC * most
    names = NY * NC * per
    keys_in = NC * own_rows

    def turn(v):
        return jnp.where(v == 0, 0, jnp.where(v == 3, 1, jnp.where(v == 1, 2, 3)))

    def back(v):
        return jnp.where(v == 0, 0, jnp.where(v == 1, 3, jnp.where(v == 2, 1, 2)))

    def spot(index, y, c):
        part = index // own_rows
        chip = (y + back(part // NC)) % NY
        core = (part + c) % NC
        return chip, core, (chip * NC + core) * own_rows + index % own_rows

    def kernel(where_ref, ids_ref, slot_ref, seen_ref):
        y, c = where_ref[0], where_ref[1]
        shape = (names, tokens)
        row = lax.broadcasted_iota(jnp.int32, shape, 0)
        chip, core, place = spot(lax.broadcasted_iota(jnp.int32, shape, 1), y, c)
        source = row // (NC * per)
        source = (y + back(source)) % NY
        kind = row % (NC * per)
        name = (source * NC + (kind // per + c) % NC) * per + kind % per
        member = ids_ref[0:1, :] == name
        for k in range(1, top):
            member = member | (ids_ref[k : k + 1, :] == name)
        a = lax.broadcasted_iota(jnp.int32, (tokens, tokens), 0)
        b = lax.broadcasted_iota(jnp.int32, (tokens, tokens), 1)
        before = ((a < b) & (a // own_rows == b // own_rows)).astype(F32).astype(BF)
        rank = jnp.dot(
            member.astype(F32).astype(BF), before, preferred_element_type=F32
        ).astype(jnp.int32)
        group = turn((chip - source + NY) % NY) * NC + (core + c) % NC
        slot = jnp.where(member, group * most + rank, -1)
        slot_ref[...] = slot[: NC * per]
        at = lax.broadcasted_iota(jnp.int32, (tokens, keys_in), 0)
        key = lax.broadcasted_iota(jnp.int32, (tokens, keys_in), 1)
        visible = spot(key, y, c)[2] <= spot(at, y, c)[2]
        visible = visible.astype(F32).astype(BF)
        level = lax.broadcasted_iota(jnp.int32, (slots, tokens), 0)
        for e in range(names):
            pick = (level == slot[e : e + 1, :]).astype(F32).astype(BF)
            seen_ref[e * slots : (e + 1) * slots, :] = jnp.dot(
                pick, visible, preferred_element_type=F32
            ).astype(BF)

    vm = pl.BlockSpec(memory_space=VM)
    return pl.pallas_call(
        kernel,
        grid_spec=pltpu.PrefetchScalarGridSpec(
            num_scalar_prefetch=1, grid=(), in_specs=[vm], out_specs=[vm, vm]
        ),
        out_shape=[
            jax.ShapeDtypeStruct((NC * per, tokens), jnp.int32),
            jax.ShapeDtypeStruct((names * slots, keys_in), BF),
        ],
        compiler_params=pltpu.CompilerParams(vmem_limit_bytes=32 << 20),
        cost_estimate=pl.CostEstimate(
            flops=2 * names * slots * tokens * keys_in, bytes_accessed=1 << 20, transcendentals=0
        ),
        name="plan",
    )(where, ids)


def split3(v):
    hi = lax.reduce_precision(v, 8, 7)
    rest = v - hi
    mid = lax.reduce_precision(rest, 8, 7)
    return jnp.stack([hi, mid, rest - mid]).astype(BF)


def pad_rows(v, rows):
    return jnp.concatenate([v, jnp.zeros((rows - v.shape[0], v.shape[1]), v.dtype)], axis=0)


def body(tokens, routes, gates, w_kv, w_query, w_out):
    per, width, hd = w_query.shape
    batch, own_rows, _ = tokens.shape
    top = routes.shape[2]
    experts = per * NC * NY
    most = max(2, 3 * own_rows * top // (2 * experts))
    block = own_rows * NC * NY
    rows = per * NC * NY * NC * most
    mine = lax.axis_index("expert")
    place = lax.axis_index("seq")
    y, c = mine // NC, mine % NC
    x, z = place // NZ, place % NZ

    near = lax.dynamic_index_in_dim(tokens, c, 0, keepdims=False)
    far = lax.dynamic_index_in_dim(tokens, 1 - c, 0, keepdims=False)

    a_own = move_expert(near, 1, 0)
    b_sib = move_expert(far, -1, 1)
    sib = move_expert(far, 0, 1)

    own_ids = lax.dynamic_slice_in_dim(routes, mine * own_rows, own_rows, 1)
    onehot = (own_ids[..., None] == jnp.arange(experts, dtype=jnp.int32)).astype(F32)
    counts = jnp.sum(onehot, axis=(0, 1, 2))
    gate_sum = jnp.sum(onehot * gates[..., None], axis=(0, 1, 2))
    stats = jnp.concatenate([counts, gate_sum])
    line = split3(stats).reshape(1, 6 * experts)
    line = jnp.concatenate([line, jnp.zeros((1, 2 * hd - 6 * experts), BF)], axis=1)

    kv2 = jnp.dot(tokens.reshape(-1, width), w_kv, preferred_element_type=F32).astype(BF)
    kv2 = kv2.reshape(batch, own_rows, 2 * hd)
    kv_near = lax.dynamic_index_in_dim(kv2, c, 0, keepdims=False)
    kv_far = lax.dynamic_index_in_dim(kv2, 1 - c, 0, keepdims=False)
    gate_far = lax.dynamic_index_in_dim(gates, 1 - c, 0, keepdims=False)
    gate_near = lax.dynamic_index_in_dim(gates, c, 0, keepdims=False)
    tail = pad_rows(split3(gate_far).reshape(3, own_rows * top), 16)
    swapped = move_expert(jnp.concatenate([kv_far, tail], axis=0), 0, 1)
    chip_gates = jnp.concatenate(
        [split3(gate_near).reshape(3, 1, -1), swapped[own_rows : own_rows + 3][:, None]], axis=1
    )
    chip_gates = pad_rows(chip_gates.reshape(-1, hd), 16)
    kv_chip = jnp.concatenate([kv_near, swapped[:own_rows], pad_rows(line, 16)], axis=0)
    x1p, x1m, x2 = move_seq(kv_chip, 1, 0), move_seq(kv_chip, -1, 0), move_seq(kv_chip, 2, 0)
    x1p, x1m, x2, sib, a_own, b_sib, routes, near, far, w_query = lax.optimization_barrier(
        (x1p, x1m, x2, sib, a_own, b_sib, routes, near, far, w_query)
    )
    ax = jnp.stack([kv_chip, x1p, x1m, x2])
    a1p, a1m = move_seq(ax, 0, 1), move_seq(ax, 0, -1)
    a_sib = move_expert(far, 1, 1)
    b_own = move_expert(near, -1, 0)
    wq_sib = move_expert(w_query, 0, 1)
    a1p, a1m, a_sib, b_own, wq_sib, a_own, b_sib, w_out = lax.optimization_barrier(
        (a1p, a1m, a_sib, b_own, wq_sib, a_own, b_sib, w_out)
    )
    a2p, a2m = move_seq(a1p, 0, 1), move_seq(a1m, 0, -1)
    d_own = move_expert(a_own, 1, 0)
    d_sib = move_expert(b_sib, -1, 0)
    wo_sib = move_expert(w_out, 0, 1)
    q0 = project([near, sib], w_query, wq_sib)
    a2p, a2m, d_own, d_sib, wo_sib, q0, a_sib = lax.optimization_barrier(
        (a2p, a2m, d_own, d_sib, wo_sib, q0, a_sib)
    )
    a3p, a3m = move_seq(a2p, 0, 1), move_seq(a2m, 0, -1)
    q1 = project([a_own, a_sib, b_own, b_sib], w_query, wq_sib)
    a3p, a3m, q1, d_own = lax.optimization_barrier((a3p, a3m, q1, d_own))
    a4p, a4m = move_seq(a3p[:2], 0, 1), move_seq(a3m[2:], 0, -1)
    pieces = [ax, a1p, a1m, a2p, a2m, a3p, a3m, a4p, a4m]
    keys_in = NC * own_rows

    zs = (0, -1, 1, -2, 2, -3, 3, 4)
    xs = (0, -1, 1, 2)
    rel = [(i, k) for k in zs for i in xs]
    rel_x = jnp.array([r[0] for r in rel], jnp.int32)
    rel_z = jnp.array([r[1] for r in rel], jnp.int32)
    where = ((x + rel_x + NX) % NX) * NZ + (z + rel_z + NZ) % NZ
    blocks = len(rel)
    past = (where < place).astype(jnp.int32)
    index = jnp.arange(blocks, dtype=jnp.int32)
    rank = jnp.sum(jnp.where(index[None, :] < index[:, None], past[None, :], 0), axis=1)
    hit = (rank[None, :] == index[:, None]) & (past[None, :] > 0)
    order = jnp.sum(jnp.where(hit, index[None, :], 0), axis=1)
    order = jnp.concatenate([order, place.astype(jnp.int32).reshape(1)])

    cores = jnp.stack([c, 1 - c]).astype(jnp.int32)
    turn = (y + jnp.array([0, 3, 1, 2], jnp.int32)) % NY
    part = (turn[:, None] * NC + cores).reshape(-1)
    routes_c = lax.dynamic_index_in_dim(routes, c, 0, keepdims=False)
    ids = routes_c.reshape(NY * NC, own_rows, top)[part].reshape(block, top)
    slot_id, seen = plan(jnp.stack([y, c]).astype(jnp.int32), ids.T, per, own_rows, most)
    names = (y * NC + cores)[:, None] * per + jnp.arange(per, dtype=jnp.int32)
    names = names.reshape(-1)

    queries = [q0, q1, project([d_own, d_sib], w_query, wq_sib)]
    q_own = compact(queries, slot_id, chip_gates, most)
    q_all = [q_own, move_expert(q_own, 1, 0), move_expert(q_own, -1, 0), move_expert(q_own, 2, 0)]
    done = attention(order, q_all, seen, pieces, rows, keys_in)
    done = [
        done[0],
        move_expert(done[1], -1, 0),
        move_expert(done[2], 1, 0),
        move_expert(done[3], 2, 0),
    ]

    got_gates = jnp.stack([q[rows:].astype(F32)[: 3 * NC * own_rows * top // hd] for q in q_all])
    got_gates = jnp.sum(got_gates.reshape(NY, 3, -1), axis=1)
    gates_c = got_gates.reshape(block, top)
    match = ids[:, None, :] == names[None, :, None]
    gate = jnp.sum(jnp.where(match, gates_c[:, None, :], 0.0), axis=2)
    notes = jnp.stack([d[rows + 24 : rows + 30].astype(F32) for d in done])
    notes = jnp.sum(notes.reshape(-1, 2 * hd), axis=0)
    heads = merge(done, slot_id, gate, most)

    o_own, o_sib, l_own, l_sib, u_own, u_sib, p_own, p_sib = expand(heads, 0, 8, w_out, wo_sib)
    relay_up = move_expert(p_own, 1, 0)
    relay_down = move_expert(p_sib, -1, 0)
    got_up_far = move_expert(u_sib, 1, 1)
    got_down_near = move_expert(l_own, -1, 0)
    got_far = move_expert(o_sib, 0, 1)
    relay_up, relay_down, got_far, notes = lax.optimization_barrier(
        (relay_up, relay_down, got_far, notes)
    )
    stats = jnp.sum(notes[: 6 * experts].reshape(3, 2 * experts), axis=0).reshape(1, -1)
    stats = stats + move_expert(stats, 0, 1)
    u_sum = (u_own.astype(F32) + relay_up.astype(F32)).astype(BF)
    l_sum = (l_sib.astype(F32) + relay_down.astype(F32)).astype(BF)
    got_up_near = move_expert(u_sum, 1, 0)
    got_down_far = move_expert(l_sum, -1, 1)
    out_near = o_own.astype(F32) + got_up_near.astype(F32) + got_down_near.astype(F32)
    out_far = got_far.astype(F32) + got_up_far.astype(F32) + got_down_far.astype(F32)
    mixed = jnp.stack(
        [jnp.where(c == 0, out_near, out_far), jnp.where(c == 0, out_far, out_near)]
    ).astype(BF)

    stats = stats.reshape(-1)
    tokens_all = batch * block * NX * NZ
    balance = experts * jnp.sum(
        stats[:experts] / (tokens_all * top) * (stats[experts:] / tokens_all)
    )
    return (mixed, balance)


def solution(mesh):
    return jax.shard_map(
        body,
        mesh=mesh,
        in_specs=(
            P(None, ("seq", "expert"), None),
            P(None, "seq", None),
            P(None, ("seq", "expert"), None),
            P(),
            P("expert", None, None),
            P("expert", None, None),
        ),
        out_specs=(P(None, ("seq", "expert"), None), P()),
        check_vma=False,
    )
```

```python
import functools
import math

import jax
import jax.numpy as jnp
from jax import lax
from jax.experimental import pallas as pl
from jax.experimental.pallas import tpu as pltpu
from jax.sharding import PartitionSpec as P

BF = jnp.bfloat16
F32 = jnp.float32
VM = pltpu.VMEM
NX, NZ = 4, 8
NY, NC = 4, 2
NT = (((1,), (1,)), ((), ()))
TN = (((0,), (0,)), ((), ()))


def move_expert(v, step, flip):
    pairs = [
        (y * NC + c, ((y + step) % NY) * NC + (c ^ flip))
        for y in range(NY)
        for c in range(NC)
    ]
    return lax.ppermute(v, "expert", pairs)


def move_seq(v, dx, dz):
    pairs = [
        (x * NZ + z, ((x + dx) % NX) * NZ + (z + dz) % NZ)
        for x in range(NX)
        for z in range(NZ)
    ]
    return lax.ppermute(v, "seq", pairs)


def project(chunks, w_own, w_sib):
    rows = sum(c.shape[0] for c in chunks)
    width = chunks[0].shape[1]
    per, _, hd = w_own.shape
    n = len(chunks)

    def kernel(*refs):
        x = jnp.concatenate([r[...] for r in refs[:n]], axis=0)
        w = jnp.concatenate([refs[n][0], refs[n + 1][0]], axis=1)
        refs[n + 2][...] = jnp.dot(x, w, preferred_element_type=F32).astype(BF)

    return pl.pallas_call(
        kernel,
        grid=(per,),
        out_shape=jax.ShapeDtypeStruct((rows, 2 * per * hd), BF),
        in_specs=[pl.BlockSpec(c.shape, lambda i: (0, 0)) for c in chunks]
        + [pl.BlockSpec((1, width, hd), lambda i: (i, 0, 0))] * 2,
        out_specs=pl.BlockSpec((rows, 2 * hd), lambda i: (0, i)),
        compiler_params=pltpu.CompilerParams(vmem_limit_bytes=60 << 20),
        cost_estimate=pl.CostEstimate(
            flops=2 * rows * width * 2 * per * hd,
            bytes_accessed=2 * (rows * width + 2 * per * hd * width),
            transcendentals=0,
        ),
        name="project",
    )(*chunks, w_own, w_sib)


def expand(heads, first, pieces, w_own, w_sib, tile=1024, piece=64):
    per, hd, width = w_own.shape
    rows = piece * pieces

    def kernel(h_ref, wo_ref, ws_ref, *outs):
        h = h_ref[...]
        wo = wo_ref[...].reshape(per * hd, tile)
        ws = ws_ref[...].reshape(per * hd, tile)
        out = jnp.dot(h[:, : per * hd], wo, preferred_element_type=F32)
        out = out + jnp.dot(h[:, per * hd :], ws, preferred_element_type=F32)
        out = out.astype(BF)
        for k, ref in enumerate(outs):
            ref[...] = out[k * piece : (k + 1) * piece]

    return pl.pallas_call(
        kernel,
        grid=(width // tile,),
        out_shape=[jax.ShapeDtypeStruct((piece, width), BF)] * pieces,
        in_specs=[pl.BlockSpec((rows, 2 * per * hd), lambda i: (first, 0))]
        + [pl.BlockSpec((per, hd, tile), lambda i: (0, 0, i))] * 2,
        out_specs=[pl.BlockSpec((piece, tile), lambda i: (0, i))] * pieces,
        compiler_params=pltpu.CompilerParams(vmem_limit_bytes=60 << 20),
        cost_estimate=pl.CostEstimate(
            flops=2 * rows * width * 2 * per * hd,
            bytes_accessed=2 * (rows * width + 2 * per * hd * width),
            transcendentals=0,
        ),
        name="expand",
    )(heads, w_own, w_sib)


def compact(queries, slot_id, extra, most):
    n_q = len(queries)
    experts, tokens = slot_id.shape
    slots = 8 * most
    rows = experts * slots
    hd = queries[0].shape[1] // experts

    def kernel(*refs):
        q_refs = refs[:n_q]
        slot_ref, extra_ref, out_ref = refs[n_q:]
        level = lax.broadcasted_iota(jnp.int32, (slots, tokens), 0)
        for e in range(experts):
            pick = (level == slot_ref[e : e + 1, :]).astype(BF)
            col = (2 * e if e < experts // 2 else 2 * (e - experts // 2) + 1) * hd
            q = jnp.concatenate([r[:, col : col + hd] for r in q_refs], axis=0)
            out_ref[e * slots : (e + 1) * slots, :] = jnp.dot(
                pick, q, preferred_element_type=F32
            ).astype(BF)
        out_ref[rows:, :] = extra_ref[...]

    vm = pl.BlockSpec(memory_space=VM)
    return pl.pallas_call(
        kernel,
        out_shape=jax.ShapeDtypeStruct((rows + extra.shape[0], hd), BF),
        in_specs=[vm] * (n_q + 2),
        out_specs=vm,
        compiler_params=pltpu.CompilerParams(vmem_limit_bytes=60 << 20),
        cost_estimate=pl.CostEstimate(
            flops=2 * rows * tokens * hd, bytes_accessed=4 << 20, transcendentals=0
        ),
        name="compact",
    )(*queries, slot_id, extra)


def attention(order, queries, seen, pieces, rows, keys_in, tile=384, group=4):
    n_q = len(queries)
    n_p = len(pieces)
    hd = pieces[0].shape[-1] // 2
    blocks = sum(p.shape[0] for p in pieces)
    total = n_q * rows
    coef = math.log2(math.e) / math.sqrt(hd)
    lines = rows // hd

    def kernel(order_ref, *refs):
        q_refs = refs[:n_q]
        seen_ref = refs[n_q]
        piece_refs = refs[n_q + 1 : n_q + 1 + n_p]
        outs = refs[n_q + 1 + n_p : 2 * n_q + 1 + n_p]
        kv, tails, q_s, m_s, acc_s, sem, tail_sem = refs[2 * n_q + 1 + n_p :]
        copies = []
        late = []
        base = 0
        for k, ref in enumerate(piece_refs):
            size = ref.shape[0]
            copies.append(
                pltpu.make_async_copy(
                    ref.at[:, :keys_in, :], kv.at[base : base + size], sem.at[k]
                )
            )
            late.append(
                pltpu.make_async_copy(
                    ref.at[:, keys_in:, :], tails.at[base : base + size], tail_sem.at[k]
                )
            )
            base += size
        for copy in copies + late:
            copy.start()
        for k, ref in enumerate(q_refs):
            q_s[k * rows : (k + 1) * rows, :] = ref[:rows, :]
        for copy in copies:
            copy.wait()

        def fold(index, first):
            n = len(index)
            got = [kv[i] for i in index]
            keys = jnp.concatenate([a[:, :hd] for a in got], axis=0)
            vals = jnp.concatenate([a[:, hd:] for a in got], axis=0)
            vals = jnp.concatenate([vals, jnp.ones(vals.shape, BF)], axis=1)

            def several(t):
                if True:
                    at = pl.ds(t * tile, tile)
                    s = lax.dot_general(
                        q_s[at, :], keys, NT, preferred_element_type=F32
                    )
                    if first:
                        mask = seen_ref[at, :].astype(F32) > 0.5
                        head = jnp.where(mask, s[:, :keys_in], -1e30)
                        s = jnp.concatenate([head, s[:, keys_in:]], axis=1) if n > 1 else head
                    top = jnp.max(s, axis=1, keepdims=True)
                    if first:
                        new = jnp.broadcast_to(top, (tile, hd))
                    else:
                        old = m_s[at, :]
                        new = jnp.maximum(old, top)
                    wide = jnp.concatenate([new] * (n * keys_in // hd), axis=1)
                    p = jnp.exp2((s - wide) * coef)
                    if first:
                        head = jnp.where(mask, p[:, :keys_in], 0.0)
                        p = jnp.concatenate([head, p[:, keys_in:]], axis=1) if n > 1 else head
                    part = jnp.dot(p.astype(BF), vals, preferred_element_type=F32)
                    if not first:
                        decay = jnp.exp2((old - new) * coef)
                        part = part + acc_s[at, :] * jnp.concatenate([decay, decay], axis=1)
                    acc_s[at, :] = part
                    m_s[at, :] = new

            for t in range(total // tile):
                several(t)

        count = order_ref[blocks]
        extra = count % group
        for n in range(group):

            @pl.when(extra == n)
            def _(n=n):
                fold([0] + [order_ref[k] for k in range(n)], True)

        def step(i, carry):
            at = extra + i * group
            fold([order_ref[at + k] for k in range(group)], False)
            return carry

        lax.fori_loop(0, count // group, step, 0)

        eye = lax.broadcasted_iota(jnp.int32, (hd, hd), 0) == lax.broadcasted_iota(
            jnp.int32, (hd, hd), 1
        )
        which = lax.broadcasted_iota(jnp.int32, (8, hd), 0)
        for copy in late:
            copy.wait()
        sums = tails[0].astype(F32)
        for i in range(1, blocks):
            sums = sums + tails[i].astype(F32)
        sums = jnp.sum(sums, axis=0, keepdims=True)
        top = sums.astype(BF).astype(F32)
        mid = (sums - top).astype(BF).astype(F32)
        low = sums - top - mid
        note = jnp.zeros((8, hd), F32)
        for i, v in enumerate((top, mid, low)):
            note = jnp.where(which == 2 * i, v[:, :hd], note)
            note = jnp.where(which == 2 * i + 1, v[:, hd:], note)
        for k, ref in enumerate(outs):
            a = acc_s[k * rows : (k + 1) * rows, :]
            m = m_s[k * rows : (k + 1) * rows, :]
            amount = a[:, hd:]
            some = amount > 0.0
            safe = jnp.where(some, amount, 1.0)
            ref[:rows, :] = jnp.where(some, a[:, :hd] / safe, 0.0).astype(BF)
            level = jnp.where(some, m * coef + jnp.log2(safe), -1e30)
            flat = jnp.zeros((8, hd), F32)
            for i in range(lines):
                line = jnp.sum(
                    jnp.where(eye, level[i * hd : (i + 1) * hd, :], 0.0), axis=0, keepdims=True
                )
                flat = jnp.where(which == i, line, flat)
            hi = flat.astype(BF).astype(F32)
            mid = (flat - hi).astype(BF).astype(F32)
            low = flat - hi - mid
            ref[rows:, :] = jnp.concatenate([hi, mid, low, note], axis=0).astype(BF)

    vm = pl.BlockSpec(memory_space=VM)
    return pl.pallas_call(
        kernel,
        grid_spec=pltpu.PrefetchScalarGridSpec(
            num_scalar_prefetch=1,
            grid=(),
            in_specs=[vm] * (n_q + 1) + [pl.BlockSpec(memory_space=pl.ANY)] * n_p,
            out_specs=[vm] * n_q,
            scratch_shapes=[
                VM((blocks, keys_in, 2 * hd), BF),
                VM((blocks, pieces[0].shape[1] - keys_in, 2 * hd), BF),
                VM((total, hd), BF),
                VM((total, hd), F32),
                VM((total, 2 * hd), F32),
                pltpu.SemaphoreType.DMA((n_p,)),
                pltpu.SemaphoreType.DMA((n_p,)),
            ],
        ),
        out_shape=[jax.ShapeDtypeStruct((rows + 32, hd), BF)] * n_q,
        compiler_params=pltpu.CompilerParams(vmem_limit_bytes=60 << 20),
        cost_estimate=pl.CostEstimate(
            flops=total * blocks * keys_in * hd * 4,
            bytes_accessed=blocks * keys_in * hd * 4,
            transcendentals=total * blocks * keys_in,
        ),
        name="attention",
    )(order, *queries, seen, *pieces)


def merge(parts, slot_id, gate, most):
    n_q = len(parts)
    experts, tokens = slot_id.shape
    slots = 8 * most
    rows = experts * slots
    hd = parts[0].shape[1]
    lines = rows // hd

    def kernel(*refs):
        p_refs = refs[:n_q]
        slot_ref, gate_ref, out_ref, heads = refs[n_q:]
        eye = lax.broadcasted_iota(jnp.int32, (hd, hd), 0) == lax.broadcasted_iota(
            jnp.int32, (hd, hd), 1
        )
        levels = []
        for r in p_refs:
            tail = r[rows:, :].astype(F32)
            levels.append(tail[0:8] + tail[8:16] + tail[16:24])
        best = functools.reduce(jnp.maximum, levels)
        share = [jnp.exp2(v - best) for v in levels]
        amount = functools.reduce(jnp.add, share)
        share = [v / amount for v in share]
        for i in range(lines):
            at = slice(i * hd, (i + 1) * hd)
            out = jnp.zeros((hd, hd), F32)
            for r, v in zip(p_refs, share):
                w = jnp.sum(jnp.where(eye, v[i : i + 1, :], 0.0), axis=1, keepdims=True)
                out = out + w * r[at, :].astype(F32)
            heads[at, :] = out.astype(BF)
        level = lax.broadcasted_iota(jnp.int32, (slots, tokens), 0)
        for e in range(experts):
            pick = (level == slot_ref[e : e + 1, :]).astype(BF)
            spread = lax.dot_general(
                pick, heads[e * slots : (e + 1) * slots, :], TN, preferred_element_type=F32
            )
            out_ref[:, e * hd : (e + 1) * hd] = (spread * gate_ref[:, e : e + 1]).astype(BF)

    vm = pl.BlockSpec(memory_space=VM)
    return pl.pallas_call(
        kernel,
        out_shape=jax.ShapeDtypeStruct((tokens, experts * hd), BF),
        in_specs=[vm] * (n_q + 2),
        out_specs=vm,
        scratch_shapes=[VM((rows, hd), BF)],
        compiler_params=pltpu.CompilerParams(vmem_limit_bytes=16 << 20),
        cost_estimate=pl.CostEstimate(
            flops=2 * rows * tokens * hd, bytes_accessed=4 << 20, transcendentals=0
        ),
        name="merge",
    )(*parts, slot_id, gate)


def plan(where, ids, per, own_rows, most):
    top, tokens = ids.shape
    slots = NY * NC * most
    names = NY * NC * per
    keys_in = NC * own_rows

    def turn(v):
        return jnp.where(v == 0, 0, jnp.where(v == 3, 1, jnp.where(v == 1, 2, 3)))

    def back(v):
        return jnp.where(v == 0, 0, jnp.where(v == 1, 3, jnp.where(v == 2, 1, 2)))

    def spot(index, y, c):
        part = index // own_rows
        chip = (y + back(part // NC)) % NY
        core = (part + c) % NC
        return chip, core, (chip * NC + core) * own_rows + index % own_rows

    def kernel(where_ref, ids_ref, slot_ref, seen_ref):
        y, c = where_ref[0], where_ref[1]
        shape = (names, tokens)
        row = lax.broadcasted_iota(jnp.int32, shape, 0)
        chip, core, place = spot(lax.broadcasted_iota(jnp.int32, shape, 1), y, c)
        source = row // (NC * per)
        source = (y + back(source)) % NY
        kind = row % (NC * per)
        name = (source * NC + (kind // per + c) % NC) * per + kind % per
        member = ids_ref[0:1, :] == name
        for k in range(1, top):
            member = member | (ids_ref[k : k + 1, :] == name)
        a = lax.broadcasted_iota(jnp.int32, (tokens, tokens), 0)
        b = lax.broadcasted_iota(jnp.int32, (tokens, tokens), 1)
        before = ((a < b) & (a // own_rows == b // own_rows)).astype(F32).astype(BF)
        rank = jnp.dot(
            member.astype(F32).astype(BF), before, preferred_element_type=F32
        ).astype(jnp.int32)
        group = turn((chip - source + NY) % NY) * NC + (core + c) % NC
        slot = jnp.where(member, group * most + rank, -1)
        slot_ref[...] = slot[: NC * per]
        at = lax.broadcasted_iota(jnp.int32, (tokens, keys_in), 0)
        key = lax.broadcasted_iota(jnp.int32, (tokens, keys_in), 1)
        visible = spot(key, y, c)[2] <= spot(at, y, c)[2]
        visible = visible.astype(F32).astype(BF)
        level = lax.broadcasted_iota(jnp.int32, (slots, tokens), 0)
        for e in range(names):
            pick = (level == slot[e : e + 1, :]).astype(F32).astype(BF)
            seen_ref[e * slots : (e + 1) * slots, :] = jnp.dot(
                pick, visible, preferred_element_type=F32
            ).astype(BF)

    vm = pl.BlockSpec(memory_space=VM)
    return pl.pallas_call(
        kernel,
        grid_spec=pltpu.PrefetchScalarGridSpec(
            num_scalar_prefetch=1, grid=(), in_specs=[vm], out_specs=[vm, vm]
        ),
        out_shape=[
            jax.ShapeDtypeStruct((NC * per, tokens), jnp.int32),
            jax.ShapeDtypeStruct((names * slots, keys_in), BF),
        ],
        compiler_params=pltpu.CompilerParams(vmem_limit_bytes=32 << 20),
        cost_estimate=pl.CostEstimate(
            flops=2 * names * slots * tokens * keys_in, bytes_accessed=1 << 20, transcendentals=0
        ),
        name="plan",
    )(where, ids)


def split3(v):
    hi = lax.reduce_precision(v, 8, 7)
    rest = v - hi
    mid = lax.reduce_precision(rest, 8, 7)
    return jnp.stack([hi, mid, rest - mid]).astype(BF)


def pad_rows(v, rows):
    return jnp.concatenate([v, jnp.zeros((rows - v.shape[0], v.shape[1]), v.dtype)], axis=0)


def body(tokens, routes, gates, w_kv, w_query, w_out):
    per, width, hd = w_query.shape
    batch, own_rows, _ = tokens.shape
    top = routes.shape[2]
    experts = per * NC * NY
    most = max(2, 3 * own_rows * top // (2 * experts))
    block = own_rows * NC * NY
    rows = per * NC * NY * NC * most
    mine = lax.axis_index("expert")
    place = lax.axis_index("seq")
    y, c = mine // NC, mine % NC
    x, z = place // NZ, place % NZ

    near = lax.dynamic_index_in_dim(tokens, c, 0, keepdims=False)
    far = lax.dynamic_index_in_dim(tokens, 1 - c, 0, keepdims=False)

    a_own = move_expert(near, 1, 0)
    b_sib = move_expert(far, -1, 1)
    sib = move_expert(far, 0, 1)

    own_ids = lax.dynamic_slice_in_dim(routes, mine * own_rows, own_rows, 1)
    onehot = (own_ids[..., None] == jnp.arange(experts, dtype=jnp.int32)).astype(F32)
    counts = jnp.sum(onehot, axis=(0, 1, 2))
    gate_sum = jnp.sum(onehot * gates[..., None], axis=(0, 1, 2))
    stats = jnp.concatenate([counts, gate_sum])
    line = split3(stats).reshape(1, 6 * experts)
    line = jnp.concatenate([line, jnp.zeros((1, 2 * hd - 6 * experts), BF)], axis=1)

    kv2 = jnp.dot(tokens.reshape(-1, width), w_kv, preferred_element_type=F32).astype(BF)
    kv2 = kv2.reshape(batch, own_rows, 2 * hd)
    kv_near = lax.dynamic_index_in_dim(kv2, c, 0, keepdims=False)
    kv_far = lax.dynamic_index_in_dim(kv2, 1 - c, 0, keepdims=False)
    gate_far = lax.dynamic_index_in_dim(gates, 1 - c, 0, keepdims=False)
    gate_near = lax.dynamic_index_in_dim(gates, c, 0, keepdims=False)
    tail = pad_rows(split3(gate_far).reshape(3, own_rows * top), 16)
    swapped = move_expert(jnp.concatenate([kv_far, tail], axis=0), 0, 1)
    chip_gates = jnp.concatenate(
        [split3(gate_near).reshape(3, 1, -1), swapped[own_rows : own_rows + 3][:, None]], axis=1
    )
    chip_gates = pad_rows(chip_gates.reshape(-1, hd), 16)
    kv_chip = jnp.concatenate([kv_near, swapped[:own_rows], pad_rows(line, 16)], axis=0)
    x1p, x1m, x2 = move_seq(kv_chip, 1, 0), move_seq(kv_chip, -1, 0), move_seq(kv_chip, 2, 0)
    x1p, x1m, x2, sib, a_own, b_sib, routes, near, far, w_query = lax.optimization_barrier(
        (x1p, x1m, x2, sib, a_own, b_sib, routes, near, far, w_query)
    )
    ax = jnp.stack([kv_chip, x1p, x1m, x2])
    a1p, a1m = move_seq(ax, 0, 1), move_seq(ax, 0, -1)
    a_sib = move_expert(far, 1, 1)
    b_own = move_expert(near, -1, 0)
    wq_sib = move_expert(w_query, 0, 1)
    a1p, a1m, a_sib, b_own, wq_sib, a_own, b_sib, w_out = lax.optimization_barrier(
        (a1p, a1m, a_sib, b_own, wq_sib, a_own, b_sib, w_out)
    )
    a2p, a2m = move_seq(a1p, 0, 1), move_seq(a1m, 0, -1)
    d_own = move_expert(a_own, 1, 0)
    d_sib = move_expert(b_sib, -1, 0)
    wo_sib = move_expert(w_out, 0, 1)
    q0 = project([near, sib], w_query, wq_sib)
    q1 = project([a_own, a_sib, b_own, b_sib], w_query, wq_sib)
    a2p, a2m, d_own, d_sib, wo_sib, q0, q1, routes = lax.optimization_barrier(
        (a2p, a2m, d_own, d_sib, wo_sib, q0, q1, routes)
    )
    cores = jnp.stack([c, 1 - c]).astype(jnp.int32)
    turn = (y + jnp.array([0, 3, 1, 2], jnp.int32)) % NY
    part = (turn[:, None] * NC + cores).reshape(-1)
    routes_c = lax.dynamic_index_in_dim(routes, c, 0, keepdims=False)
    ids = routes_c.reshape(NY * NC, own_rows, top)[part].reshape(block, top)
    slot_id, seen = plan(jnp.stack([y, c]).astype(jnp.int32), ids.T, per, own_rows, most)
    names = (y * NC + cores)[:, None] * per + jnp.arange(per, dtype=jnp.int32)
    names = names.reshape(-1)

    a3p, a3m = move_seq(a2p, 0, 1), move_seq(a2m, 0, -1)
    queries = [q0, q1, project([d_own, d_sib], w_query, wq_sib)]
    q_own = compact(queries, slot_id, chip_gates, most)
    a3p, a3m, q_own = lax.optimization_barrier((a3p, a3m, q_own))
    a4p, a4m = move_seq(a3p[:2], 0, 1), move_seq(a3m[2:], 0, -1)
    pieces = [ax, a1p, a1m, a2p, a2m, a3p, a3m, a4p, a4m]
    keys_in = NC * own_rows

    zs = (0, -1, 1, -2, 2, -3, 3, 4)
    xs = (0, -1, 1, 2)
    rel = [(i, k) for k in zs for i in xs]
    rel_x = jnp.array([r[0] for r in rel], jnp.int32)
    rel_z = jnp.array([r[1] for r in rel], jnp.int32)
    where = ((x + rel_x + NX) % NX) * NZ + (z + rel_z + NZ) % NZ
    blocks = len(rel)
    past = (where < place).astype(jnp.int32)
    index = jnp.arange(blocks, dtype=jnp.int32)
    rank = jnp.sum(jnp.where(index[None, :] < index[:, None], past[None, :], 0), axis=1)
    hit = (rank[None, :] == index[:, None]) & (past[None, :] > 0)
    order = jnp.sum(jnp.where(hit, index[None, :], 0), axis=1)
    order = jnp.concatenate([order, place.astype(jnp.int32).reshape(1)])

    q_all = [q_own, move_expert(q_own, 1, 0), move_expert(q_own, -1, 0), move_expert(q_own, 2, 0)]
    done = attention(order, q_all, seen, pieces, rows, keys_in)
    done = [
        done[0],
        move_expert(done[1], -1, 0),
        move_expert(done[2], 1, 0),
        move_expert(done[3], 2, 0),
    ]

    got_gates = jnp.stack([q[rows:].astype(F32)[: 3 * NC * own_rows * top // hd] for q in q_all])
    got_gates = jnp.sum(got_gates.reshape(NY, 3, -1), axis=1)
    gates_c = got_gates.reshape(block, top)
    match = ids[:, None, :] == names[None, :, None]
    gate = jnp.sum(jnp.where(match, gates_c[:, None, :], 0.0), axis=2)
    notes = jnp.stack([d[rows + 24 : rows + 30].astype(F32) for d in done])
    notes = jnp.sum(notes.reshape(-1, 2 * hd), axis=0)
    heads = merge(done, slot_id, gate, most)

    o_own, o_sib, l_own, l_sib, u_own, u_sib, p_own, p_sib = expand(heads, 0, 8, w_out, wo_sib)
    relay_up = move_expert(p_own, 1, 0)
    relay_down = move_expert(p_sib, -1, 0)
    got_up_far = move_expert(u_sib, 1, 1)
    got_down_near = move_expert(l_own, -1, 0)
    got_far = move_expert(o_sib, 0, 1)
    relay_up, relay_down, got_far, notes = lax.optimization_barrier(
        (relay_up, relay_down, got_far, notes)
    )
    stats = jnp.sum(notes[: 6 * experts].reshape(3, 2 * experts), axis=0).reshape(1, -1)
    stats = stats + move_expert(stats, 0, 1)
    u_sum = (u_own.astype(F32) + relay_up.astype(F32)).astype(BF)
    l_sum = (l_sib.astype(F32) + relay_down.astype(F32)).astype(BF)
    got_up_near = move_expert(u_sum, 1, 0)
    got_down_far = move_expert(l_sum, -1, 1)
    out_near = o_own.astype(F32) + got_up_near.astype(F32) + got_down_near.astype(F32)
    out_far = got_far.astype(F32) + got_up_far.astype(F32) + got_down_far.astype(F32)
    mixed = jnp.stack(
        [jnp.where(c == 0, out_near, out_far), jnp.where(c == 0, out_far, out_near)]
    ).astype(BF)

    stats = stats.reshape(-1)
    tokens_all = batch * block * NX * NZ
    balance = experts * jnp.sum(
        stats[:experts] / (tokens_all * top) * (stats[experts:] / tokens_all)
    )
    return (mixed, balance)


def solution(mesh):
    return jax.shard_map(
        body,
        mesh=mesh,
        in_specs=(
            P(None, ("seq", "expert"), None),
            P(None, "seq", None),
            P(None, ("seq", "expert"), None),
            P(),
            P("expert", None, None),
            P("expert", None, None),
        ),
        out_specs=(P(None, ("seq", "expert"), None), P()),
        check_vma=False,
    )
```

```python
import functools
import math

import jax
import jax.numpy as jnp
from jax import lax
from jax.experimental import pallas as pl
from jax.experimental.pallas import tpu as pltpu
from jax.sharding import PartitionSpec as P

BF = jnp.bfloat16
F32 = jnp.float32
VM = pltpu.VMEM
NX, NZ = 4, 8
NY, NC = 4, 2
NT = (((1,), (1,)), ((), ()))
TN = (((0,), (0,)), ((), ()))


def move_expert(v, step, flip):
    pairs = [
        (y * NC + c, ((y + step) % NY) * NC + (c ^ flip))
        for y in range(NY)
        for c in range(NC)
    ]
    return lax.ppermute(v, "expert", pairs)


def move_seq(v, dx, dz):
    pairs = [
        (x * NZ + z, ((x + dx) % NX) * NZ + (z + dz) % NZ)
        for x in range(NX)
        for z in range(NZ)
    ]
    return lax.ppermute(v, "seq", pairs)


def project(chunks, w_own, w_sib):
    rows = sum(c.shape[0] for c in chunks)
    width = chunks[0].shape[1]
    per, _, hd = w_own.shape
    n = len(chunks)

    def kernel(*refs):
        x = jnp.concatenate([r[...] for r in refs[:n]], axis=0)
        w = jnp.concatenate([refs[n][0], refs[n + 1][0]], axis=1)
        refs[n + 2][...] = jnp.dot(x, w, preferred_element_type=F32).astype(BF)

    return pl.pallas_call(
        kernel,
        grid=(per,),
        out_shape=jax.ShapeDtypeStruct((rows, 2 * per * hd), BF),
        in_specs=[pl.BlockSpec(c.shape, lambda i: (0, 0)) for c in chunks]
        + [pl.BlockSpec((1, width, hd), lambda i: (i, 0, 0))] * 2,
        out_specs=pl.BlockSpec((rows, 2 * hd), lambda i: (0, i)),
        compiler_params=pltpu.CompilerParams(vmem_limit_bytes=60 << 20),
        cost_estimate=pl.CostEstimate(
            flops=2 * rows * width * 2 * per * hd,
            bytes_accessed=2 * (rows * width + 2 * per * hd * width),
            transcendentals=0,
        ),
        name="project",
    )(*chunks, w_own, w_sib)


def expand(heads, first, pieces, w_own, w_sib, tile=1024, piece=64):
    per, hd, width = w_own.shape
    rows = piece * pieces

    def kernel(h_ref, wo_ref, ws_ref, *outs):
        h = h_ref[...]
        wo = wo_ref[...].reshape(per * hd, tile)
        ws = ws_ref[...].reshape(per * hd, tile)
        w = jnp.concatenate([wo, ws], axis=0)
        out = jnp.dot(h, w, preferred_element_type=F32).astype(BF)
        for k, ref in enumerate(outs):
            ref[...] = out[k * piece : (k + 1) * piece]

    return pl.pallas_call(
        kernel,
        grid=(width // tile,),
        out_shape=[jax.ShapeDtypeStruct((piece, width), BF)] * pieces,
        in_specs=[pl.BlockSpec((rows, 2 * per * hd), lambda i: (first, 0))]
        + [pl.BlockSpec((per, hd, tile), lambda i: (0, 0, i))] * 2,
        out_specs=[pl.BlockSpec((piece, tile), lambda i: (0, i))] * pieces,
        compiler_params=pltpu.CompilerParams(vmem_limit_bytes=60 << 20),
        cost_estimate=pl.CostEstimate(
            flops=2 * rows * width * 2 * per * hd,
            bytes_accessed=2 * (rows * width + 2 * per * hd * width),
            transcendentals=0,
        ),
        name="expand",
    )(heads, w_own, w_sib)


def compact(queries, slot_id, extra, most):
    n_q = len(queries)
    experts, tokens = slot_id.shape
    slots = 8 * most
    rows = experts * slots
    hd = queries[0].shape[1] // experts

    def kernel(*refs):
        q_refs = refs[:n_q]
        slot_ref, extra_ref, out_ref = refs[n_q:]
        level = lax.broadcasted_iota(jnp.int32, (slots, tokens), 0)
        for e in range(experts):
            pick = (level == slot_ref[e : e + 1, :]).astype(BF)
            col = (2 * e if e < experts // 2 else 2 * (e - experts // 2) + 1) * hd
            q = jnp.concatenate([r[:, col : col + hd] for r in q_refs], axis=0)
            out_ref[e * slots : (e + 1) * slots, :] = jnp.dot(
                pick, q, preferred_element_type=F32
            ).astype(BF)
        out_ref[rows:, :] = extra_ref[...]

    vm = pl.BlockSpec(memory_space=VM)
    return pl.pallas_call(
        kernel,
        out_shape=jax.ShapeDtypeStruct((rows + extra.shape[0], hd), BF),
        in_specs=[vm] * (n_q + 2),
        out_specs=vm,
        compiler_params=pltpu.CompilerParams(vmem_limit_bytes=60 << 20),
        cost_estimate=pl.CostEstimate(
            flops=2 * rows * tokens * hd, bytes_accessed=4 << 20, transcendentals=0
        ),
        name="compact",
    )(*queries, slot_id, extra)


def attention(order, queries, seen, pieces, rows, keys_in, tile=384, group=4):
    n_q = len(queries)
    n_p = len(pieces)
    hd = pieces[0].shape[-1] // 2
    blocks = sum(p.shape[0] for p in pieces)
    total = n_q * rows
    coef = math.log2(math.e) / math.sqrt(hd)
    lines = rows // hd

    def kernel(order_ref, *refs):
        q_refs = refs[:n_q]
        seen_ref = refs[n_q]
        piece_refs = refs[n_q + 1 : n_q + 1 + n_p]
        outs = refs[n_q + 1 + n_p : 2 * n_q + 1 + n_p]
        kv, tails, q_s, m_s, acc_s, sem, tail_sem = refs[2 * n_q + 1 + n_p :]
        copies = []
        late = []
        base = 0
        for k, ref in enumerate(piece_refs):
            size = ref.shape[0]
            copies.append(
                pltpu.make_async_copy(
                    ref.at[:, :keys_in, :], kv.at[base : base + size], sem.at[k]
                )
            )
            late.append(
                pltpu.make_async_copy(
                    ref.at[:, keys_in:, :], tails.at[base : base + size], tail_sem.at[k]
                )
            )
            base += size
        for copy in copies + late:
            copy.start()
        for k, ref in enumerate(q_refs):
            q_s[k * rows : (k + 1) * rows, :] = ref[:rows, :]
        for copy in copies:
            copy.wait()

        def fold(index, first):
            n = len(index)
            got = [kv[i] for i in index]
            keys = jnp.concatenate([a[:, :hd] for a in got], axis=0)
            vals = jnp.concatenate([a[:, hd:] for a in got], axis=0)
            vals = jnp.concatenate([vals, jnp.ones(vals.shape, BF)], axis=1)

            def several(t):
                if True:
                    at = pl.ds(t * tile, tile)
                    s = lax.dot_general(
                        q_s[at, :], keys, NT, preferred_element_type=F32
                    )
                    if first:
                        mask = seen_ref[at, :].astype(F32) > 0.5
                        head = jnp.where(mask, s[:, :keys_in], -1e30)
                        s = jnp.concatenate([head, s[:, keys_in:]], axis=1) if n > 1 else head
                    top = jnp.max(s, axis=1, keepdims=True)
                    if first:
                        new = jnp.broadcast_to(top, (tile, hd))
                    else:
                        old = m_s[at, :]
                        new = jnp.maximum(old, top)
                    wide = jnp.concatenate([new] * (n * keys_in // hd), axis=1)
                    p = jnp.exp2((s - wide) * coef)
                    if first:
                        head = jnp.where(mask, p[:, :keys_in], 0.0)
                        p = jnp.concatenate([head, p[:, keys_in:]], axis=1) if n > 1 else head
                    part = jnp.dot(p.astype(BF), vals, preferred_element_type=F32)
                    if not first:
                        decay = jnp.exp2((old - new) * coef)
                        part = part + acc_s[at, :] * jnp.concatenate([decay, decay], axis=1)
                    acc_s[at, :] = part
                    m_s[at, :] = new

            for t in range(total // tile):
                several(t)

        count = order_ref[blocks]
        extra = count % group
        for n in range(group):

            @pl.when(extra == n)
            def _(n=n):
                fold([0] + [order_ref[k] for k in range(n)], True)

        def step(i, carry):
            at = extra + i * group
            fold([order_ref[at + k] for k in range(group)], False)
            return carry

        lax.fori_loop(0, count // group, step, 0)

        eye = lax.broadcasted_iota(jnp.int32, (hd, hd), 0) == lax.broadcasted_iota(
            jnp.int32, (hd, hd), 1
        )
        which = lax.broadcasted_iota(jnp.int32, (8, hd), 0)
        for copy in late:
            copy.wait()
        sums = tails[0].astype(F32)
        for i in range(1, blocks):
            sums = sums + tails[i].astype(F32)
        sums = jnp.sum(sums, axis=0, keepdims=True)
        top = sums.astype(BF).astype(F32)
        mid = (sums - top).astype(BF).astype(F32)
        low = sums - top - mid
        note = jnp.zeros((8, hd), F32)
        for i, v in enumerate((top, mid, low)):
            note = jnp.where(which == 2 * i, v[:, :hd], note)
            note = jnp.where(which == 2 * i + 1, v[:, hd:], note)
        for k, ref in enumerate(outs):
            a = acc_s[k * rows : (k + 1) * rows, :]
            m = m_s[k * rows : (k + 1) * rows, :]
            amount = a[:, hd:]
            some = amount > 0.0
            safe = jnp.where(some, amount, 1.0)
            ref[:rows, :] = jnp.where(some, a[:, :hd] / safe, 0.0).astype(BF)
            level = jnp.where(some, m * coef + jnp.log2(safe), -1e30)
            flat = jnp.zeros((8, hd), F32)
            for i in range(lines):
                line = jnp.sum(
                    jnp.where(eye, level[i * hd : (i + 1) * hd, :], 0.0), axis=0, keepdims=True
                )
                flat = jnp.where(which == i, line, flat)
            hi = flat.astype(BF).astype(F32)
            mid = (flat - hi).astype(BF).astype(F32)
            low = flat - hi - mid
            ref[rows:, :] = jnp.concatenate([hi, mid, low, note], axis=0).astype(BF)

    vm = pl.BlockSpec(memory_space=VM)
    return pl.pallas_call(
        kernel,
        grid_spec=pltpu.PrefetchScalarGridSpec(
            num_scalar_prefetch=1,
            grid=(),
            in_specs=[vm] * (n_q + 1) + [pl.BlockSpec(memory_space=pl.ANY)] * n_p,
            out_specs=[vm] * n_q,
            scratch_shapes=[
                VM((blocks, keys_in, 2 * hd), BF),
                VM((blocks, pieces[0].shape[1] - keys_in, 2 * hd), BF),
                VM((total, hd), BF),
                VM((total, hd), F32),
                VM((total, 2 * hd), F32),
                pltpu.SemaphoreType.DMA((n_p,)),
                pltpu.SemaphoreType.DMA((n_p,)),
            ],
        ),
        out_shape=[jax.ShapeDtypeStruct((rows + 32, hd), BF)] * n_q,
        compiler_params=pltpu.CompilerParams(vmem_limit_bytes=60 << 20),
        cost_estimate=pl.CostEstimate(
            flops=total * blocks * keys_in * hd * 4,
            bytes_accessed=blocks * keys_in * hd * 4,
            transcendentals=total * blocks * keys_in,
        ),
        name="attention",
    )(order, *queries, seen, *pieces)


def merge(parts, slot_id, gate, most):
    n_q = len(parts)
    experts, tokens = slot_id.shape
    slots = 8 * most
    rows = experts * slots
    hd = parts[0].shape[1]
    lines = rows // hd

    def kernel(*refs):
        p_refs = refs[:n_q]
        slot_ref, gate_ref, out_ref, heads = refs[n_q:]
        eye = lax.broadcasted_iota(jnp.int32, (hd, hd), 0) == lax.broadcasted_iota(
            jnp.int32, (hd, hd), 1
        )
        levels = []
        for r in p_refs:
            tail = r[rows:, :].astype(F32)
            levels.append(tail[0:8] + tail[8:16] + tail[16:24])
        best = functools.reduce(jnp.maximum, levels)
        share = [jnp.exp2(v - best) for v in levels]
        amount = functools.reduce(jnp.add, share)
        share = [v / amount for v in share]
        for i in range(lines):
            at = slice(i * hd, (i + 1) * hd)
            out = jnp.zeros((hd, hd), F32)
            for r, v in zip(p_refs, share):
                w = jnp.sum(jnp.where(eye, v[i : i + 1, :], 0.0), axis=1, keepdims=True)
                out = out + w * r[at, :].astype(F32)
            heads[at, :] = out.astype(BF)
        level = lax.broadcasted_iota(jnp.int32, (slots, tokens), 0)
        for e in range(experts):
            pick = (level == slot_ref[e : e + 1, :]).astype(BF)
            spread = lax.dot_general(
                pick, heads[e * slots : (e + 1) * slots, :], TN, preferred_element_type=F32
            )
            out_ref[:, e * hd : (e + 1) * hd] = (spread * gate_ref[:, e : e + 1]).astype(BF)

    vm = pl.BlockSpec(memory_space=VM)
    return pl.pallas_call(
        kernel,
        out_shape=jax.ShapeDtypeStruct((tokens, experts * hd), BF),
        in_specs=[vm] * (n_q + 2),
        out_specs=vm,
        scratch_shapes=[VM((rows, hd), BF)],
        compiler_params=pltpu.CompilerParams(vmem_limit_bytes=16 << 20),
        cost_estimate=pl.CostEstimate(
            flops=2 * rows * tokens * hd, bytes_accessed=4 << 20, transcendentals=0
        ),
        name="merge",
    )(*parts, slot_id, gate)


def plan(where, ids, per, own_rows, most):
    top, tokens = ids.shape
    slots = NY * NC * most
    names = NY * NC * per
    keys_in = NC * own_rows

    def turn(v):
        return jnp.where(v == 0, 0, jnp.where(v == 3, 1, jnp.where(v == 1, 2, 3)))

    def back(v):
        return jnp.where(v == 0, 0, jnp.where(v == 1, 3, jnp.where(v == 2, 1, 2)))

    def spot(index, y, c):
        part = index // own_rows
        chip = (y + back(part // NC)) % NY
        core = (part + c) % NC
        return chip, core, (chip * NC + core) * own_rows + index % own_rows

    def kernel(where_ref, ids_ref, slot_ref, seen_ref):
        y, c = where_ref[0], where_ref[1]
        shape = (names, tokens)
        row = lax.broadcasted_iota(jnp.int32, shape, 0)
        chip, core, place = spot(lax.broadcasted_iota(jnp.int32, shape, 1), y, c)
        source = row // (NC * per)
        source = (y + back(source)) % NY
        kind = row % (NC * per)
        name = (source * NC + (kind // per + c) % NC) * per + kind % per
        member = ids_ref[0:1, :] == name
        for k in range(1, top):
            member = member | (ids_ref[k : k + 1, :] == name)
        a = lax.broadcasted_iota(jnp.int32, (tokens, tokens), 0)
        b = lax.broadcasted_iota(jnp.int32, (tokens, tokens), 1)
        before = ((a < b) & (a // own_rows == b // own_rows)).astype(F32).astype(BF)
        rank = jnp.dot(
            member.astype(F32).astype(BF), before, preferred_element_type=F32
        ).astype(jnp.int32)
        group = turn((chip - source + NY) % NY) * NC + (core + c) % NC
        slot = jnp.where(member, group * most + rank, -1)
        slot_ref[...] = slot[: NC * per]
        at = lax.broadcasted_iota(jnp.int32, (tokens, keys_in), 0)
        key = lax.broadcasted_iota(jnp.int32, (tokens, keys_in), 1)
        visible = spot(key, y, c)[2] <= spot(at, y, c)[2]
        visible = visible.astype(F32).astype(BF)
        level = lax.broadcasted_iota(jnp.int32, (slots, tokens), 0)
        for e in range(names):
            pick = (level == slot[e : e + 1, :]).astype(F32).astype(BF)
            seen_ref[e * slots : (e + 1) * slots, :] = jnp.dot(
                pick, visible, preferred_element_type=F32
            ).astype(BF)

    vm = pl.BlockSpec(memory_space=VM)
    return pl.pallas_call(
        kernel,
        grid_spec=pltpu.PrefetchScalarGridSpec(
            num_scalar_prefetch=1, grid=(), in_specs=[vm], out_specs=[vm, vm]
        ),
        out_shape=[
            jax.ShapeDtypeStruct((NC * per, tokens), jnp.int32),
            jax.ShapeDtypeStruct((names * slots, keys_in), BF),
        ],
        compiler_params=pltpu.CompilerParams(vmem_limit_bytes=32 << 20),
        cost_estimate=pl.CostEstimate(
            flops=2 * names * slots * tokens * keys_in, bytes_accessed=1 << 20, transcendentals=0
        ),
        name="plan",
    )(where, ids)


def split3(v):
    hi = lax.reduce_precision(v, 8, 7)
    rest = v - hi
    mid = lax.reduce_precision(rest, 8, 7)
    return jnp.stack([hi, mid, rest - mid]).astype(BF)


def pad_rows(v, rows):
    return jnp.concatenate([v, jnp.zeros((rows - v.shape[0], v.shape[1]), v.dtype)], axis=0)


def body(tokens, routes, gates, w_kv, w_query, w_out):
    per, width, hd = w_query.shape
    batch, own_rows, _ = tokens.shape
    top = routes.shape[2]
    experts = per * NC * NY
    most = max(2, 3 * own_rows * top // (2 * experts))
    block = own_rows * NC * NY
    rows = per * NC * NY * NC * most
    mine = lax.axis_index("expert")
    place = lax.axis_index("seq")
    y, c = mine // NC, mine % NC
    x, z = place // NZ, place % NZ

    near = lax.dynamic_index_in_dim(tokens, c, 0, keepdims=False)
    far = lax.dynamic_index_in_dim(tokens, 1 - c, 0, keepdims=False)

    a_own = move_expert(near, 1, 0)
    b_sib = move_expert(far, -1, 1)
    sib = move_expert(far, 0, 1)

    own_ids = lax.dynamic_slice_in_dim(routes, mine * own_rows, own_rows, 1)
    onehot = (own_ids[..., None] == jnp.arange(experts, dtype=jnp.int32)).astype(F32)
    counts = jnp.sum(onehot, axis=(0, 1, 2))
    gate_sum = jnp.sum(onehot * gates[..., None], axis=(0, 1, 2))
    stats = jnp.concatenate([counts, gate_sum])
    line = split3(stats).reshape(1, 6 * experts)
    line = jnp.concatenate([line, jnp.zeros((1, 2 * hd - 6 * experts), BF)], axis=1)

    kv2 = jnp.dot(tokens.reshape(-1, width), w_kv, preferred_element_type=F32).astype(BF)
    kv2 = kv2.reshape(batch, own_rows, 2 * hd)
    kv_near = lax.dynamic_index_in_dim(kv2, c, 0, keepdims=False)
    kv_far = lax.dynamic_index_in_dim(kv2, 1 - c, 0, keepdims=False)
    gate_far = lax.dynamic_index_in_dim(gates, 1 - c, 0, keepdims=False)
    gate_near = lax.dynamic_index_in_dim(gates, c, 0, keepdims=False)
    tail = pad_rows(split3(gate_far).reshape(3, own_rows * top), 16)
    swapped = move_expert(jnp.concatenate([kv_far, tail], axis=0), 0, 1)
    chip_gates = jnp.concatenate(
        [split3(gate_near).reshape(3, 1, -1), swapped[own_rows : own_rows + 3][:, None]], axis=1
    )
    chip_gates = pad_rows(chip_gates.reshape(-1, hd), 16)
    kv_chip = jnp.concatenate([kv_near, swapped[:own_rows], pad_rows(line, 16)], axis=0)
    x1p, x1m, x2 = move_seq(kv_chip, 1, 0), move_seq(kv_chip, -1, 0), move_seq(kv_chip, 2, 0)
    x1p, x1m, x2, sib, a_own, b_sib, routes, near, far, w_query = lax.optimization_barrier(
        (x1p, x1m, x2, sib, a_own, b_sib, routes, near, far, w_query)
    )
    ax = jnp.stack([kv_chip, x1p, x1m, x2])
    a1p, a1m = move_seq(ax, 0, 1), move_seq(ax, 0, -1)
    a_sib = move_expert(far, 1, 1)
    b_own = move_expert(near, -1, 0)
    wq_sib = move_expert(w_query, 0, 1)
    a1p, a1m, a_sib, b_own, wq_sib, a_own, b_sib, w_out = lax.optimization_barrier(
        (a1p, a1m, a_sib, b_own, wq_sib, a_own, b_sib, w_out)
    )
    a2p, a2m = move_seq(a1p, 0, 1), move_seq(a1m, 0, -1)
    d_own = move_expert(a_own, 1, 0)
    d_sib = move_expert(b_sib, -1, 0)
    wo_sib = move_expert(w_out, 0, 1)
    q0 = project([near, sib, a_own, a_sib, b_own, b_sib], w_query, wq_sib)
    a2p, a2m, d_own, d_sib, wo_sib, q0, routes = lax.optimization_barrier(
        (a2p, a2m, d_own, d_sib, wo_sib, q0, routes)
    )
    cores = jnp.stack([c, 1 - c]).astype(jnp.int32)
    turn = (y + jnp.array([0, 3, 1, 2], jnp.int32)) % NY
    part = (turn[:, None] * NC + cores).reshape(-1)
    routes_c = lax.dynamic_index_in_dim(routes, c, 0, keepdims=False)
    ids = routes_c.reshape(NY * NC, own_rows, top)[part].reshape(block, top)
    slot_id, seen = plan(jnp.stack([y, c]).astype(jnp.int32), ids.T, per, own_rows, most)
    names = (y * NC + cores)[:, None] * per + jnp.arange(per, dtype=jnp.int32)
    names = names.reshape(-1)

    a3p, a3m = move_seq(a2p, 0, 1), move_seq(a2m, 0, -1)
    queries = [q0, project([d_own, d_sib], w_query, wq_sib)]
    q_own = compact(queries, slot_id, chip_gates, most)
    a3p, a3m, q_own = lax.optimization_barrier((a3p, a3m, q_own))
    a4p, a4m = move_seq(a3p[:2], 0, 1), move_seq(a3m[2:], 0, -1)
    pieces = [ax, a1p, a1m, a2p, a2m, a3p, a3m, a4p, a4m]
    keys_in = NC * own_rows

    zs = (0, -1, 1, -2, 2, -3, 3, 4)
    xs = (0, -1, 1, 2)
    rel = [(i, k) for k in zs for i in xs]
    rel_x = jnp.array([r[0] for r in rel], jnp.int32)
    rel_z = jnp.array([r[1] for r in rel], jnp.int32)
    where = ((x + rel_x + NX) % NX) * NZ + (z + rel_z + NZ) % NZ
    blocks = len(rel)
    past = (where < place).astype(jnp.int32)
    index = jnp.arange(blocks, dtype=jnp.int32)
    rank = jnp.sum(jnp.where(index[None, :] < index[:, None], past[None, :], 0), axis=1)
    hit = (rank[None, :] == index[:, None]) & (past[None, :] > 0)
    order = jnp.sum(jnp.where(hit, index[None, :], 0), axis=1)
    order = jnp.concatenate([order, place.astype(jnp.int32).reshape(1)])

    q_all = [q_own, move_expert(q_own, 1, 0), move_expert(q_own, -1, 0), move_expert(q_own, 2, 0)]
    done = attention(order, q_all, seen, pieces, rows, keys_in)
    done = [
        done[0],
        move_expert(done[1], -1, 0),
        move_expert(done[2], 1, 0),
        move_expert(done[3], 2, 0),
    ]

    got_gates = jnp.stack([q[rows:].astype(F32)[: 3 * NC * own_rows * top // hd] for q in q_all])
    got_gates = jnp.sum(got_gates.reshape(NY, 3, -1), axis=1)
    gates_c = got_gates.reshape(block, top)
    match = ids[:, None, :] == names[None, :, None]
    gate = jnp.sum(jnp.where(match, gates_c[:, None, :], 0.0), axis=2)
    notes = jnp.stack([d[rows + 24 : rows + 30].astype(F32) for d in done])
    notes = jnp.sum(notes.reshape(-1, 2 * hd), axis=0)
    heads = merge(done, slot_id, gate, most)

    o_own, o_sib, l_own, l_sib, u_own, u_sib, p_own, p_sib = expand(heads, 0, 8, w_out, wo_sib)
    relay_up = move_expert(p_own, 1, 0)
    relay_down = move_expert(p_sib, -1, 0)
    got_up_far = move_expert(u_sib, 1, 1)
    got_down_near = move_expert(l_own, -1, 0)
    got_far = move_expert(o_sib, 0, 1)
    relay_up, relay_down, got_far, notes = lax.optimization_barrier(
        (relay_up, relay_down, got_far, notes)
    )
    stats = jnp.sum(notes[: 6 * experts].reshape(3, 2 * experts), axis=0).reshape(1, -1)
    stats = stats + move_expert(stats, 0, 1)
    u_sum = (u_own.astype(F32) + relay_up.astype(F32)).astype(BF)
    l_sum = (l_sib.astype(F32) + relay_down.astype(F32)).astype(BF)
    got_up_near = move_expert(u_sum, 1, 0)
    got_down_far = move_expert(l_sum, -1, 1)
    out_near = o_own.astype(F32) + got_up_near.astype(F32) + got_down_near.astype(F32)
    out_far = got_far.astype(F32) + got_up_far.astype(F32) + got_down_far.astype(F32)
    mixed = jnp.stack(
        [jnp.where(c == 0, out_near, out_far), jnp.where(c == 0, out_far, out_near)]
    ).astype(BF)

    stats = stats.reshape(-1)
    tokens_all = batch * block * NX * NZ
    balance = experts * jnp.sum(
        stats[:experts] / (tokens_all * top) * (stats[experts:] / tokens_all)
    )
    return (mixed, balance)


def solution(mesh):
    return jax.shard_map(
        body,
        mesh=mesh,
        in_specs=(
            P(None, ("seq", "expert"), None),
            P(None, "seq", None),
            P(None, ("seq", "expert"), None),
            P(),
            P("expert", None, None),
            P("expert", None, None),
        ),
        out_specs=(P(None, ("seq", "expert"), None), P()),
        check_vma=False,
    )
```
